32 devices in a mesh: groups: 2 (over y), req: 4 (over z), head: 4 (over x, core).
Axes of the slice: x: 2, y: 2, z: 4, core: 2. Of those that a mesh axis runs over, the one named last changes fastest.
Arguments:
- prompt_states: bfloat16 [4096, 8192], P(('groups', 'req'), 'head'), parts along dimension 0, may hold values from -6 to 6
- norm_gain: bfloat16 [8192], replicated, may hold values from 0.099609375 to 1.8984375
- key_weight: bfloat16 [8192, 1024], P('req', 'head'), may hold values from -0.0625 to 0.0625
- value_weight: bfloat16 [8192, 1024], P('req', 'head'), may hold values from -0.0625 to 0.0625
- block_owner: int32 [512, 1], P(('groups', 'req')), parts along dimension 0, may hold values from 0 to 3; in each aligned block of 64 rows (0 to 63, 64 to 127, ...) at most 22 rows name the same one
- block_slot: int32 [512], P(('groups', 'req')), parts along dimension 0, may hold values from 0 to 1
- block_len: int32 [512], P(('groups', 'req')), parts along dimension 0, may hold values from 1 to 8
- cache_key: bfloat16 [16, 1024, 1024], P(('groups', 'req'), None, 'head'), parts along dimension 0
- cache_value: bfloat16 [16, 1024, 1024], P(('groups', 'req'), None, 'head'), parts along dimension 0, may hold values from -6 to 6
- cache_len: int32 [16], P(('groups', 'req')), parts along dimension 0, may hold values from 2 to 1024
- query: bfloat16 [16, 2, 8192], P(('groups', 'req'), None, 'head'), parts along dimension 0
- step_key: bfloat16 [16, 2, 1024], P(('groups', 'req'), None, 'head'), parts along dimension 0, may hold values from -6 to 6
- step_value: bfloat16 [16, 2, 1024], P(('groups', 'req'), None, 'head'), parts along dimension 0, may hold values from -6 to 6
- out_weight: bfloat16 [8192, 8192], P('head', 'req'), may hold values from -0.0625 to 0.0625
Outputs:
- decoded: bfloat16 [16, 2, 8192], P(('groups', 'head'), None, 'req'), parts along dimension 0
The draws below stay inside these ranges and needn't reach their ends.
There are 2 independent parts, one for each index of `groups`. The reference program is written for one: setup_inputs(seed, part) draws one part's arguments, and reference() takes and returns one part's arrays. A program takes and returns all parts, laid end to end along the dimension named above; an argument that names none is the same for every part. Nothing has to cross between parts.
Inputs may be any that keep to these rules, and one draw needn't show every extreme that they name: `block_owner`: among the 64 blocks of one index of req no decode index is named more than 22 times, a bound that some block reaches.
All inputs are finite; a program needn't handle non-finite values.
Results may differ from the reference program's by a relative error of at most 0.0095.
Values may be sent and summed in bfloat16 or wider, within the bound.
A program may use at most 128 MiB of HBM per device.

```python
import math
import jax
import jax.numpy as jnp
import numpy as np
from jax import lax

D = 8192
KVH = 8
QPK = 8
HD = 128
BLK = 8
STEPS = 2
REQ_DEV = 2
CACHE = 1024
BLOCKS_DEV = 64
BLOCKS = 256
PRE_TOTAL = 2048
NREQ = 8
CAPB = 22
N_REQ = 4


def shared_keys(key):
    return jax.random.normal(key, (NREQ, CACHE, KVH * HD), jnp.float32)


def draw_cache_key(key, part):
    base = shared_keys(key)
    return jnp.clip(base, -6.0, 6.0).astype(jnp.bfloat16)


def draw_query(key, part):
    key = jax.random.fold_in(key, 12)
    own = jax.random.normal(key, (NREQ, STEPS, KVH * QPK * HD), jnp.float32)
    return jnp.clip(own, -6.0, 6.0).astype(jnp.bfloat16)


def place_ends(array, key, low, high):
    dims = array.shape
    spot = [jax.random.randint(jax.random.fold_in(key, axis), (), 0, dims[axis]) for axis in range(len(dims))]
    array = array.at[tuple(spot)].set(low)
    longest = dims.index(max(dims))
    spot[longest] = (spot[longest] + 1) % dims[longest]
    return array.at[tuple(spot)].set(high)


def block_levels(rng, shape, pieces, smallest, high):
    loudness, own = 1.0, jax.random.fold_in(rng, 6)
    for dim, shards_of in pieces:
        heights = jnp.exp(jax.random.uniform(jax.random.fold_in(own, dim), (shards_of,), jnp.float32, smallest / len(pieces), high / len(pieces)))
        loudness = loudness * jnp.repeat(heights, shape[dim] // shards_of).reshape([-1 if axis == dim else 1 for axis in range(len(shape))])
    return loudness


def shared_out(rng, own, number, rows, count, top, reach, skew):
    order = jax.random.permutation(rng, count)
    heavy_load, common = load_shares(count, rows * top, reach, skew, True), load_shares(count, rows * top, reach, skew, False)
    places = jnp.arange(count)

    def named(tallies, offset_by):
        used = int((tallies > 0).sum())
        fixed = max(1, used // 4)
        shifted = fixed + (places - fixed + offset_by * (used - fixed)) % max(1, count - fixed)
        return jnp.zeros((count,), jnp.int32).at[order[jnp.where(places < fixed, places, shifted)]].set(jnp.asarray(tallies, jnp.int32))

    tallies = jnp.where(number % 4 == 0, named(heavy_load, number // 4), named(common, number - number // 4 - 1))
    mixed = jax.random.permutation(jax.random.fold_in(own, 3), count)
    giver, taker = mixed[0:count // 2 * 2:2], mixed[1:count // 2 * 2:2]
    slack = jnp.minimum(tallies[giver] - 1, reach - tallies[taker]) // 2
    slack = jnp.where((giver == order[0]) | (taker == order[0]) | (tallies[taker] == 0), 0, jnp.maximum(slack, 0))
    shifted = jax.random.randint(jax.random.fold_in(own, 4), (count // 2,), 0, 1 << 20) % (slack + 1)
    tallies = tallies.at[giver].add(-shifted).at[taker].add(shifted)
    labels = jnp.searchsorted(jnp.cumsum(tallies), jnp.arange(rows * top), side="right").astype(jnp.int32)
    listing = labels.reshape(top, rows).T
    listing = listing[jax.random.permutation(jax.random.fold_in(own, 1), rows)]
    offset_by = jax.random.randint(jax.random.fold_in(own, 2), (rows, 1), 0, top)
    return jnp.take_along_axis(listing, (jnp.arange(top)[None, :] + offset_by) % top, axis=1)


def load_shares(amount, total, reach, lean, full):
    weights = [(1 << 20) // math.isqrt(rank ** lean) + 1 for rank in range(1, amount + 1)]
    largest = reach if full else min(reach, max(-(-total // amount), total * weights[0] // sum(weights)))
    least = 1 if total - largest >= amount - 1 else 0
    given, spare = [largest] + [least] * (amount - 1), total - largest - least * (amount - 1)
    while spare > 0:
        candidates = [i for i in range(1, amount) if given[i] < largest] or [i for i in range(1, amount) if given[i] < reach]
        whole, budget = sum([weights[i] for i in candidates]), spare
        for i in candidates:
            more = min(reach - given[i], max(1, budget * weights[i] // whole), spare)
            given[i] = given[i] + more
            spare = spare - more
    return np.array(given)


def scatter_about(rng, extent, scale, limit, pieces=(), kind=jnp.bfloat16):
    array = jax.random.normal(rng, extent, jnp.float32) * scale
    if len(pieces) > 0:
        array = block_levels(rng, extent, pieces, -0.22, 0.18) * array
    return jnp.clip(array, min=-limit, max=limit).astype(kind)


def setup_inputs(seed: int = 0, part: int = 0) -> dict:
    key_list = jax.random.split(jax.random.key(seed), 15)
    own_keys = jax.random.split(jax.random.fold_in(key_list[14], part), 15)
    prompt_states = scatter_about(own_keys[0], (PRE_TOTAL, D), 1.0, 6.0, ((0, 4), (1, 4)))
    norm_gain = jnp.clip(1.0 + 0.18 * jax.random.normal(key_list[1], (D,), jnp.float32), 0.099609375, 1.8984375).astype(jnp.bfloat16)
    key_weight = scatter_about(key_list[2], (D, KVH * HD), D ** -0.5, 0.0625, ((0, 4), (1, 4)))
    value_weight = scatter_about(key_list[3], (D, KVH * HD), D ** -0.5, 0.0625, ((0, 4), (1, 4)))
    block_owner_keys = jax.random.split(jax.random.fold_in(own_keys[4], 1), BLOCKS // BLOCKS_DEV)
    block_owner_turns = jax.random.permutation(jax.random.fold_in(own_keys[4], 3), BLOCKS // BLOCKS_DEV)
    block_owner = jax.vmap(lambda own, number: shared_out(jax.random.fold_in(own_keys[4], 2), own, number, BLOCKS_DEV, N_REQ, 1, CAPB, 1))(block_owner_keys, block_owner_turns).reshape((BLOCKS, 1))
    block_slot = place_ends(jax.random.randint(own_keys[5], (BLOCKS,), 0, REQ_DEV), jax.random.fold_in(own_keys[5], 1), 0, REQ_DEV - 1).astype(jnp.int32)
    block_len = place_ends(jax.random.randint(own_keys[6], (BLOCKS,), 1, BLK + 1), jax.random.fold_in(own_keys[6], 1), 1, BLK).astype(jnp.int32)
    cache_key = draw_cache_key(jax.random.fold_in(jax.random.fold_in(key_list[14], part), 71), part)
    cache_value = scatter_about(own_keys[8], (NREQ, CACHE, KVH * HD), 1.0, 6.0, ((0, 4), (2, 4)))
    cache_len = place_ends(jax.random.randint(own_keys[9], (NREQ,), 2, CACHE + 1), jax.random.fold_in(own_keys[9], 1), 2, CACHE).astype(jnp.int32)
    query = draw_query(jax.random.fold_in(jax.random.fold_in(key_list[14], part), 71), part)
    step_key = scatter_about(own_keys[11], (NREQ, STEPS, KVH * HD), 1.0, 6.0, ((0, 4), (2, 4)))
    step_value = scatter_about(own_keys[12], (NREQ, STEPS, KVH * HD), 1.0, 6.0, ((0, 4), (2, 4)))
    out_weight = scatter_about(key_list[13], (KVH * QPK * HD, D), (KVH * QPK * HD) ** -0.5, 0.0625, ((0, 4), (1, 4)))
    return {"prompt_states": prompt_states, "norm_gain": norm_gain, "key_weight": key_weight, "value_weight": value_weight, "block_owner": block_owner, "block_slot": block_slot, "block_len": block_len, "cache_key": cache_key, "cache_value": cache_value, "cache_len": cache_len, "query": query, "step_key": step_key, "step_value": step_value, "out_weight": out_weight}


NEGATIVE = -1e+30

def reference(prompt_states, norm_gain, key_weight, value_weight, block_owner, block_slot, block_len, cache_key, cache_value, cache_len, query, step_key, step_value, out_weight):
    states = prompt_states.astype(jnp.float32)
    stat = lax.optimization_barrier(jnp.mean(states * states, axis=-1, keepdims=True))
    scaled = (states * norm_gain.astype(jnp.float32)).astype(jnp.bfloat16)
    factor = lax.rsqrt(stat + 1e-05)
    new_key = (jnp.dot(scaled, key_weight, preferred_element_type=jnp.float32) * factor).astype(jnp.bfloat16)
    new_value = (jnp.dot(scaled, value_weight, preferred_element_type=jnp.float32) * factor).astype(jnp.bfloat16)
    new_key = new_key.astype(jnp.float32).reshape(PRE_TOTAL, KVH, HD)
    new_value = new_value.astype(jnp.float32).reshape(PRE_TOTAL, KVH, HD)
    target = block_owner[:, 0] * REQ_DEV + block_slot
    token_ok = (jnp.arange(BLK, dtype=jnp.int32)[None, :] < block_len[:, None]).reshape(-1)
    token_target = jnp.repeat(target, BLK)
    scale = 1.0 / HD ** 0.5
    steps_ok = jnp.arange(STEPS)[None, :] <= jnp.arange(STEPS)[:, None]

    def one(index):
        queries = query[index].astype(jnp.float32).reshape(STEPS, KVH, QPK, HD)
        keys = jnp.concatenate([cache_key[index].astype(jnp.float32).reshape(CACHE, KVH, HD), new_key, step_key[index].astype(jnp.float32).reshape(STEPS, KVH, HD)], axis=0)
        values = jnp.concatenate([cache_value[index].astype(jnp.float32).reshape(CACHE, KVH, HD), new_value, step_value[index].astype(jnp.float32).reshape(STEPS, KVH, HD)], axis=0)
        cache_ok = jnp.arange(CACHE, dtype=jnp.int32) < cache_len[index]
        fresh_ok = token_ok & (token_target == index)
        front = jnp.concatenate([cache_ok, fresh_ok])
        valid = jnp.concatenate([jnp.broadcast_to(front[None, :], (STEPS, front.shape[0])), steps_ok], axis=1)
        scores = jnp.einsum('shgd,thd->shgt', queries, keys) * scale
        valid = valid[:, None, None, :]
        masked = jnp.where(valid, scores, NEGATIVE)
        top = lax.optimization_barrier(jnp.max(masked, axis=-1, keepdims=True))
        weights = jnp.where(valid, jnp.exp(masked - top), 0.0)
        total = lax.optimization_barrier(jnp.sum(weights, axis=-1))
        mixed = jnp.einsum('shgt,thd->shgd', weights, values) / total[..., None]
        return mixed.reshape(STEPS, KVH * QPK * HD)
    attention = lax.map(one, jnp.arange(NREQ, dtype=jnp.int32)).astype(jnp.bfloat16)
    decoded = jnp.dot(attention.reshape(NREQ * STEPS, KVH * QPK * HD), out_weight, preferred_element_type=jnp.float32)
    return decoded.reshape(NREQ, STEPS, D).astype(jnp.bfloat16)
```

```python
import functools

import jax
import jax.numpy as jnp
from jax import lax
from jax.experimental import pallas as pl
from jax.experimental.pallas import tpu as pltpu
from jax.sharding import PartitionSpec as P

QPK = 8
HD = 128
BLK = 8
NEGATIVE = -1e30
MESH = pl.DeviceIdType.MESH
F32 = jnp.float32
BF16 = jnp.bfloat16


def dot_t(a, b):
    return lax.dot_general(a, b, (((1,), (1,)), ((), ())), preferred_element_type=F32)


def kernel(
    nz, nh, pieces, xpieces,
    gain_ref, code_ref, clen_ref, q_ref, sk_ref, sv_ref,
    x_hbm, wk_hbm, wv_hbm, ck_hbm, cv_hbm, ow_hbm,
    out_ref,
    xraw, xbuf, wbuf, acc, ckv, owbuf, qbuf, psend, precv, cst, asend, arecv, af, osend, orecv, sbuf,
    loc, zs, zr, ys, yr, xs, xr, cs, cr, os_, or_, qs, qr, ps, pr, as_, ar, fs, fr, ss, sr,
):
    me_g = lax.axis_index("groups")
    me = lax.axis_index("req")
    mh = lax.axis_index("head")
    chip = mh // 2
    core = mh % 2
    nx = nh // 2
    sib = chip * 2 + (1 - core)
    tokens, xc = xraw.shape
    wr, width = wk_hbm.shape
    heads = width // HD
    wp = wr // pieces
    tp = tokens // xpieces
    reqs, steps = sk_ref.shape[0], sk_ref.shape[1]
    rq = steps * QPK
    own = reqs * rq
    scale = 1.0 / HD**0.5

    def at_z(p):
        return (me_g, p, mh)

    def at_h(h):
        return (me_g, me, h)

    peer_g = (1 - me_g, me, mh)

    def remote(src, dst, ssem, rsem, dev):
        return pltpu.make_async_remote_copy(
            src_ref=src, dst_ref=dst, send_sem=ssem, recv_sem=rsem, device_id=dev, device_id_type=MESH
        )

    cpx = pltpu.make_async_copy(x_hbm, xraw, loc.at[0])
    cpk = pltpu.make_async_copy(wk_hbm, wbuf.at[me, 0], loc.at[1])
    cpv = pltpu.make_async_copy(wv_hbm, wbuf.at[me, 1], loc.at[2])
    cck = pltpu.make_async_copy(ck_hbm, ckv.at[0], loc.at[3])
    ccv = pltpu.make_async_copy(cv_hbm, ckv.at[1], loc.at[4])
    cow = pltpu.make_async_copy(ow_hbm, owbuf, loc.at[5])
    for c in (cpk, cpv, cpx, cck, ccv, cow):
        c.start()

    barrier = pltpu.get_barrier_semaphore()
    for d in range(1, nz):
        pl.semaphore_signal(barrier, inc=1, device_id=at_z(lax.rem(me + d, nz)), device_id_type=MESH)
    for d in range(1, nh):
        pl.semaphore_signal(barrier, inc=1, device_id=at_h(lax.rem(mh + d, nh)), device_id_type=MESH)
    pl.semaphore_signal(barrier, inc=1, device_id=peer_g, device_id_type=MESH)
    pl.semaphore_wait(barrier, nz + nh - 1)

    pending = []

    def begin(cond, copy):
        pending.append((cond, copy))
        if cond is None:
            copy.start()
        else:
            pl.when(cond)(copy.start)

    def zcopy(d, i, chunk):
        dr = 1 - 2 * d
        k = i % pieces
        part = wbuf.at[chunk, me_g, pl.ds(k * wp, wp)]
        return remote(part, part, zs.at[d, i], zr.at[d, i], at_z(me + dr))

    def inside(v, n):
        return jnp.logical_and(v >= 0, v < n)

    cpk.wait()
    cpv.wait()
    for k in range(pieces):
        for d in range(2):
            begin(inside(me + 1 - 2 * d, nz), zcopy(d, k, me))

    for d in range(1, nz):
        begin(None, remote(q_ref, qbuf.at[me], qs.at[d - 1], qr.at[d - 1], at_z(lax.rem(me + d, nz))))
    qbuf[me] = q_ref[...]

    cpx.wait()

    def xcopy(d, e, c):
        dr = 1 - 2 * d
        k = e % xpieces
        part = xbuf.at[c, pl.ds(k * tp, tp)]
        return remote(part, part, xs.at[d, e], xr.at[d, e], at_h(mh + 2 * dr))

    ones = jnp.ones((8, xc), BF16)
    for k in range(xpieces):
        rows = pl.ds(k * tp, tp)
        xf = xraw[rows, :].astype(F32)
        xbuf[mh, rows, :] = (xf * gain_ref[...]).astype(BF16)
        for d in range(2):
            begin(inside(chip + 1 - 2 * d, nx), xcopy(d, k, mh))
        sq = xf * xf
        hi = sq.astype(BF16)
        lo = (sq - hi.astype(F32)).astype(BF16)
        sbuf[mh, :, k * tp : (k + 1) * tp] = dot_t(ones, hi) + dot_t(ones, lo)
    begin(None, remote(xbuf.at[mh], xbuf.at[mh], os_.at[0], or_.at[0], at_h(sib)))
    for d in range(1, nh):
        begin(None, remote(sbuf.at[mh], sbuf.at[mh], ss.at[d - 1], sr.at[d - 1], at_h(lax.rem(mh + d, nh))))

    cck.wait()
    ccv.wait()
    lane = lax.broadcasted_iota(jnp.int32, (1, 128), 1)
    slots = ckv.shape[2]
    for n in range(reqs):
        skf = sk_ref[n].astype(F32)
        svf = sv_ref[n].astype(F32)
        for g in range(heads):
            cols = slice(g * HD, (g + 1) * HD)
            q = q_ref[g, n * rq : (n + 1) * rq, :]
            s = dot_t(q, ckv[0, n, :, cols]) * scale
            ok = lax.broadcasted_iota(jnp.int32, (1, slots), 1) < clen_ref[n]
            s = jnp.where(ok, s, NEGATIVE)
            m = jnp.max(s, axis=-1, keepdims=True)
            qf = q.astype(F32)
            step = lax.broadcasted_iota(jnp.int32, (rq, 1), 0) // QPK
            own_s = []
            for p in range(steps):
                t = jnp.sum(qf * skf[p : p + 1, cols], axis=-1, keepdims=True) * scale
                t = jnp.where(step >= p, t, NEGATIVE)
                own_s.append(t)
                m = jnp.maximum(m, t)
            w = jnp.where(ok, jnp.exp(s - m), 0.0)
            total = jnp.sum(w, axis=-1, keepdims=True)
            a = jnp.dot(w.astype(BF16), ckv[1, n, :, cols], preferred_element_type=F32)
            for p in range(steps):
                u = jnp.where(step >= p, jnp.exp(own_s[p] - m), 0.0)
                total = total + u
                a = a + u * svf[p : p + 1, cols]
            cst[g, n * rq : (n + 1) * rq, 0:128] = a
            cst[g, n * rq : (n + 1) * rq, 128:256] = jnp.where(lane < 64, m, total)

    count = (nz - 1) * pieces
    xcount = (nx - 1) * xpieces

    def zrelay(i):
        for d in range(2):
            dr = 1 - 2 * d
            chunk = me - dr * (1 + i // pieces)
            good = inside(chunk, nz)
            pl.when(good)(zcopy(d, i, chunk).wait_recv)
            if i + pieces < count:
                begin(jnp.logical_and(good, inside(me + dr, nz)), zcopy(d, i + pieces, chunk))
            part = wbuf.at[chunk, me_g, pl.ds((i % pieces) * wp, wp)]
            begin(good, remote(part, part, ys.at[d, i], yr.at[d, i], peer_g))

    def xrelay(e):
        for d in range(2):
            dr = 1 - 2 * d
            c = chip - dr * (1 + e // xpieces)
            good = inside(c, nx)
            h = c * 2 + core
            pl.when(good)(xcopy(d, e, h).wait_recv)
            if e + xpieces < xcount:
                begin(jnp.logical_and(good, inside(chip + dr, nx)), xcopy(d, e + xpieces, h))
            part = xbuf.at[h, pl.ds((e % xpieces) * tp, tp)]
            begin(good, remote(part, part, cs.at[d, e], cr.at[d, e], at_h(sib)))

    def states_ready():
        remote(xbuf.at[sib], xbuf.at[sib], os_.at[0], or_.at[0], at_h(sib)).wait_recv()
        for e in range(xcount):
            for d in range(2):
                c = chip - (1 - 2 * d) * (1 + e // xpieces)
                part = xbuf.at[c * 2 + 1 - core, pl.ds((e % xpieces) * tp, tp)]
                pl.when(inside(c, nx))(remote(part, part, cs.at[d, e], cr.at[d, e], at_h(sib)).wait_recv)

    def multiply(chunk, k, fresh):
        at = chunk * wr + k * wp
        if wr == xc:
            lhs = xbuf[chunk, :, k * wp : (k + 1) * wp]
        else:
            lhs = xbuf[at // xc, :, pl.ds(pl.multiple_of(at % xc, 128), wp)]
        for j in range(2):
            prod = jnp.dot(lhs, wbuf[chunk, j, pl.ds(k * wp, wp), :], preferred_element_type=F32)
            acc[j] = prod if fresh else acc[j] + prod

    def consume(u):
        if u < pieces:
            multiply(me, u, u == 0)
            return
        i = u - pieces
        for d in range(2):
            chunk = me - (1 - 2 * d) * (1 + i // pieces)

            @pl.when(inside(chunk, nz))
            def _():
                part = wbuf.at[chunk, 1 - me_g, pl.ds((i % pieces) * wp, wp)]
                remote(part, part, ys.at[d, i], yr.at[d, i], peer_g).wait_recv()
                multiply(chunk, i % pieces, False)

    xdue = [max(0, (e + 1) * 2 * count // (3 * xcount) - 1) for e in range(xcount)]
    first = min(max(xdue) + 1, count - 1)
    done = 0
    for i in range(count):
        zrelay(i)
        for e in range(xcount):
            if xdue[e] == i:
                xrelay(e)
        if i == first:
            states_ready()
        if i >= first:
            goal = (pieces + i) * (i - first + 1) // (count - first)
            while done < goal:
                consume(done)
                done += 1
    while done < pieces + count:
        consume(done)
        done += 1

    for d in range(1, nz):
        src = qbuf.at[lax.rem(me - d + nz, nz)]
        remote(src, src, qs.at[d - 1], qr.at[d - 1], at_z(lax.rem(me + d, nz))).wait_recv()
    for d in range(1, nh):
        src = sbuf.at[lax.rem(mh - d + nh, nh)]
        remote(src, src, ss.at[d - 1], sr.at[d - 1], at_h(lax.rem(mh + d, nh))).wait_recv()
    stat = sbuf[0]
    for h in range(1, nh):
        stat = stat + sbuf[h]
    factor = lax.rsqrt(stat[0:1, :] * (1.0 / (nh * xc)) + 1e-05)
    rows = nz * own
    valid = code_ref[...] == lax.broadcasted_iota(jnp.int32, (rows, 1), 0) // rq
    for g in range(heads):
        cols = slice(g * HD, (g + 1) * HD)
        q = qbuf[:, g].reshape(rows, HD)
        s = dot_t(q, acc[0, :, cols].astype(BF16)) * (factor * scale)
        s = jnp.where(valid, s, NEGATIVE)
        m = jnp.max(s, axis=-1, keepdims=True)
        w = jnp.where(valid, jnp.exp(s - m), 0.0)
        total = jnp.sum(w, axis=-1, keepdims=True)
        a = jnp.dot((w * factor).astype(BF16), acc[1, :, cols].astype(BF16), preferred_element_type=F32)
        psend[:, g, :, 0:128] = a.reshape(nz, own, HD)
        psend[:, g, :, 128:256] = jnp.where(lane < 64, m, total).reshape(nz, own, 128)
    for d in range(1, nz):
        to = lax.rem(me + d, nz)
        begin(None, remote(psend.at[to], precv.at[me], ps.at[d - 1], pr.at[d - 1], at_z(to)))
    precv[me] = psend[me]
    for d in range(1, nz):
        src = precv.at[lax.rem(me - d + nz, nz)]
        remote(src, src, ps.at[d - 1], pr.at[d - 1], at_z(lax.rem(me + d, nz))).wait_recv()

    for g in range(heads):
        parts = [cst[g]] + [precv[p, g] for p in range(nz)]
        top = parts[0][:, 128:129]
        for t in parts[1:]:
            top = jnp.maximum(top, t[:, 128:129])
        total = jnp.zeros((own, 1), F32)
        a = jnp.zeros((own, HD), F32)
        for t in parts:
            e = jnp.exp(t[:, 128:129] - top)
            total = total + e * t[:, 192:193]
            a = a + e * t[:, 0:128]
        asend[g] = (a / total).astype(BF16)
    for d in range(1, nz):
        begin(None, remote(asend, arecv.at[me], as_.at[d - 1], ar.at[d - 1], at_z(lax.rem(me + d, nz))))
    arecv[me] = asend[...]
    for d in range(1, nz):
        src = arecv.at[lax.rem(me - d + nz, nz)]
        remote(src, src, as_.at[d - 1], ar.at[d - 1], at_z(lax.rem(me + d, nz))).wait_recv()

    cow.wait()
    for g in range(heads):
        af[g * nz * own : (g + 1) * nz * own, :] = arecv[:, g].reshape(nz * own, HD).astype(F32)
    every = nz * reqs * steps
    pieces_in = [
        af[pl.ds(g * nz * own + j, every, stride=QPK), :] for g in range(heads) for j in range(QPK)
    ]
    lhs = jnp.concatenate(pieces_in, axis=1).astype(BF16)
    prod = jnp.dot(lhs, owbuf[...], preferred_element_type=F32)
    ro = every // nh
    for h in range(nh):
        osend[h] = prod[h * ro : (h + 1) * ro, :]
    for d in range(1, nh):
        to = lax.rem(mh + d, nh)
        begin(None, remote(osend.at[to], orecv.at[mh], fs.at[d - 1], fr.at[d - 1], at_h(to)))
    orecv[mh] = osend[mh]
    for d in range(1, nh):
        src = orecv.at[lax.rem(mh - d + nh, nh)]
        remote(src, src, fs.at[d - 1], fr.at[d - 1], at_h(lax.rem(mh + d, nh))).wait_recv()
    final = orecv[0]
    for h in range(1, nh):
        final = final + orecv[h]
    final = final.astype(BF16)
    for n in range(ro // steps):
        out_ref[n] = final[n * steps : (n + 1) * steps, :]

    for cond, copy in pending:
        if cond is None:
            copy.wait_send()
        else:
            pl.when(cond)(copy.wait_send)


def body(
    prompt_states, norm_gain, key_weight, value_weight, block_owner, block_slot, block_len,
    cache_key, cache_value, cache_len, query, step_key, step_value, out_weight,
):
    nz, nh = lax.axis_size("req"), lax.axis_size("head")
    tokens, xc = prompt_states.shape
    wr, width = key_weight.shape
    heads = width // HD
    reqs, steps = query.shape[0], query.shape[1]
    own = reqs * steps * QPK
    oc = out_weight.shape[1]
    slots = cache_key.shape[1]
    gain = lax.dynamic_slice(norm_gain, (lax.axis_index("head") * xc,), (xc,)).astype(F32).reshape(1, xc)
    target = block_owner[:, 0] * reqs + block_slot
    code = jnp.where(jnp.arange(BLK, dtype=jnp.int32)[None, :] < block_len[:, None], target[:, None], -1)
    code = code.reshape(1, tokens)
    q = query.reshape(reqs, steps, heads, QPK, HD).transpose(2, 0, 1, 3, 4).reshape(heads, own, HD)
    pieces = max(1, wr // 512)
    xpieces = 4
    ro = nz * reqs // nh
    zc = (nz - 1) * pieces
    xcnt = (nh // 2 - 1) * xpieces
    dma = pltpu.SemaphoreType.DMA
    vm = pl.BlockSpec(memory_space=pltpu.VMEM)
    sm = pl.BlockSpec(memory_space=pltpu.SMEM)
    hb = pl.BlockSpec(memory_space=pl.ANY)
    return pl.pallas_call(
        functools.partial(kernel, nz, nh, pieces, xpieces),
        out_shape=jax.ShapeDtypeStruct((ro, steps, oc), BF16),
        in_specs=[vm, vm, sm, vm, vm, vm, hb, hb, hb, hb, hb, hb],
        out_specs=vm,
        scratch_shapes=[
            pltpu.VMEM((tokens, xc), BF16),
            pltpu.VMEM((nh, tokens, xc), BF16),
            pltpu.VMEM((nz, 2, wr, width), BF16),
            pltpu.VMEM((2, tokens, width), F32),
            pltpu.VMEM((2, reqs, slots, width), BF16),
            pltpu.VMEM(out_weight.shape, BF16),
            pltpu.VMEM((nz, heads, own, HD), BF16),
            pltpu.VMEM((nz, heads, own, 256), F32),
            pltpu.VMEM((nz, heads, own, 256), F32),
            pltpu.VMEM((heads, own, 256), F32),
            pltpu.VMEM((heads, own, HD), BF16),
            pltpu.VMEM((nz, heads, own, HD), BF16),
            pltpu.VMEM((heads * nz * own, HD), F32),
            pltpu.VMEM((nh, ro * steps, oc), F32),
            pltpu.VMEM((nh, ro * steps, oc), F32),
            pltpu.VMEM((nh, 8, tokens), F32),
            dma((6,)),
            dma((2, zc)), dma((2, zc)), dma((2, zc)), dma((2, zc)),
            dma((2, xcnt)), dma((2, xcnt)), dma((2, xcnt)), dma((2, xcnt)),
            dma((1,)), dma((1,)),
            dma((nz - 1,)), dma((nz - 1,)), dma((nz - 1,)), dma((nz - 1,)), dma((nz - 1,)), dma((nz - 1,)),
            dma((nh - 1,)), dma((nh - 1,)), dma((nh - 1,)), dma((nh - 1,)),
        ],
        compiler_params=pltpu.CompilerParams(
            collective_id=0, has_side_effects=True, vmem_limit_bytes=52 * 1024 * 1024
        ),
    )(
        gain, code, cache_len, q, step_key, step_value,
        prompt_states, key_weight, value_weight, cache_key, cache_value, out_weight,
    )


def solution(mesh):
    placed = (
        P(("groups", "req"), "head"),
        P(),
        P("req", "head"),
        P("req", "head"),
        P(("groups", "req"), None),
        P(("groups", "req")),
        P(("groups", "req")),
        P(("groups", "req"), None, "head"),
        P(("groups", "req"), None, "head"),
        P(("groups", "req")),
        P(("groups", "req"), None, "head"),
        P(("groups", "req"), None, "head"),
        P(("groups", "req"), None, "head"),
        P("head", "req"),
    )
    return jax.shard_map(
        body,
        mesh=mesh,
        in_specs=placed,
        out_specs=P(("groups", "head"), None, "req"),
        check_vma=False,
    )
```

```python
import functools

import jax
import jax.numpy as jnp
from jax import lax
from jax.experimental import pallas as pl
from jax.experimental.pallas import tpu as pltpu
from jax.sharding import PartitionSpec as P

QPK = 8
HD = 128
BLK = 8
NEGATIVE = -1e30
MESH = pl.DeviceIdType.MESH
F32 = jnp.float32
BF16 = jnp.bfloat16


def dot_t(a, b):
    return lax.dot_general(a, b, (((1,), (1,)), ((), ())), preferred_element_type=F32)


def kernel(
    nz, nh, pieces, xpieces,
    gain_hbm, owner_hbm, slot_hbm, len_hbm, clen_hbm, query_hbm, sk_hbm, sv_hbm,
    x_hbm, wk_hbm, wv_hbm, ck_hbm, cv_hbm, ow_hbm,
    out_ref,
    gain_ref, owner_ref, slot_ref, len_ref, clen_ref, query_ref, sk_ref, sv_ref, qf_ref, q_ref,
    xraw, xbuf, wbuf, acc, ckv, owbuf, qbuf, psend, precv, cst, asend, arecv, af, osend, orecv, sbuf,
    loc, zs, zr, ys, yr, xs, xr, cs, cr, os_, or_, qs, qr, ps, pr, as_, ar, fs, fr, ss, sr,
):
    me_g = lax.axis_index("groups")
    me = lax.axis_index("req")
    mh = lax.axis_index("head")
    chip = mh // 2
    core = mh % 2
    nx = nh // 2
    sib = chip * 2 + (1 - core)
    tokens, xc = xraw.shape
    wr, width = wk_hbm.shape
    heads = width // HD
    wp = wr // pieces
    tp = tokens // xpieces
    reqs, steps = sk_ref.shape[0], sk_ref.shape[1]
    rq = steps * QPK
    own = reqs * rq
    scale = 1.0 / HD**0.5

    def at_z(p):
        return (me_g, p, mh)

    def at_h(h):
        return (me_g, me, h)

    peer_g = (1 - me_g, me, mh)

    def remote(src, dst, ssem, rsem, dev):
        return pltpu.make_async_remote_copy(
            src_ref=src, dst_ref=dst, send_sem=ssem, recv_sem=rsem, device_id=dev, device_id_type=MESH
        )

    cpx = pltpu.make_async_copy(x_hbm, xraw, loc.at[0])
    cpk = pltpu.make_async_copy(wk_hbm, wbuf.at[me, 0], loc.at[1])
    cpv = pltpu.make_async_copy(wv_hbm, wbuf.at[me, 1], loc.at[2])
    cck = pltpu.make_async_copy(ck_hbm, ckv.at[0], loc.at[3])
    ccv = pltpu.make_async_copy(cv_hbm, ckv.at[1], loc.at[4])
    cow = pltpu.make_async_copy(ow_hbm, owbuf, loc.at[5])
    small = [
        pltpu.make_async_copy(src, dst, loc.at[6 + i])
        for i, (src, dst) in enumerate(
            [
                (query_hbm, query_ref), (gain_hbm, gain_ref), (owner_hbm, owner_ref), (slot_hbm, slot_ref),
                (len_hbm, len_ref), (clen_hbm, clen_ref), (sk_hbm, sk_ref), (sv_hbm, sv_ref),
            ]
        )
    ]
    for c in (cpk, cpv, cpx, *small, cck, ccv, cow):
        c.start()

    barrier = pltpu.get_barrier_semaphore()
    for d in range(1, nz):
        pl.semaphore_signal(barrier, inc=1, device_id=at_z(lax.rem(me + d, nz)), device_id_type=MESH)
    for d in range(1, nh):
        pl.semaphore_signal(barrier, inc=1, device_id=at_h(lax.rem(mh + d, nh)), device_id_type=MESH)
    pl.semaphore_signal(barrier, inc=1, device_id=peer_g, device_id_type=MESH)
    pl.semaphore_wait(barrier, nz + nh - 1)

    pending = []

    def begin(cond, copy):
        pending.append((cond, copy))
        if cond is None:
            copy.start()
        else:
            pl.when(cond)(copy.start)

    def zcopy(d, i, chunk):
        dr = 1 - 2 * d
        k = i % pieces
        part = wbuf.at[chunk, me_g, pl.ds(k * wp, wp)]
        return remote(part, part, zs.at[d, i], zr.at[d, i], at_z(me + dr))

    def inside(v, n):
        return jnp.logical_and(v >= 0, v < n)

    cpk.wait()
    cpv.wait()
    for k in range(pieces):
        for d in range(2):
            begin(inside(me + 1 - 2 * d, nz), zcopy(d, k, me))

    small[0].wait()
    for n in range(reqs):
        both = query_ref[n].astype(F32)
        for g in range(heads):
            for j in range(QPK):
                lanes = (g * QPK + j) * HD
                qf_ref[pl.ds(g * own + n * rq + j, steps, stride=QPK), :] = both[:, lanes : lanes + HD]
    q_ref[...] = qf_ref[...].astype(BF16).reshape(heads, own, HD)
    for d in range(1, nz):
        begin(None, remote(q_ref, qbuf.at[me], qs.at[d - 1], qr.at[d - 1], at_z(lax.rem(me + d, nz))))
    qbuf[me] = q_ref[...]

    cpx.wait()
    small[1].wait()
    gain = gain_ref[pl.ds(pl.multiple_of(mh * xc, 128), xc)].astype(F32).reshape(1, xc)

    def xcopy(d, e, c):
        dr = 1 - 2 * d
        k = e % xpieces
        part = xbuf.at[c, pl.ds(k * tp, tp)]
        return remote(part, part, xs.at[d, e], xr.at[d, e], at_h(mh + 2 * dr))

    ones = jnp.ones((8, xc), BF16)
    for k in range(xpieces):
        rows = pl.ds(k * tp, tp)
        xf = xraw[rows, :].astype(F32)
        xbuf[mh, rows, :] = (xf * gain).astype(BF16)
        for d in range(2):
            begin(inside(chip + 1 - 2 * d, nx), xcopy(d, k, mh))
        sq = xf * xf
        hi = sq.astype(BF16)
        lo = (sq - hi.astype(F32)).astype(BF16)
        sbuf[mh, :, k * tp : (k + 1) * tp] = dot_t(ones, hi) + dot_t(ones, lo)
    begin(None, remote(xbuf.at[mh], xbuf.at[mh], os_.at[0], or_.at[0], at_h(sib)))
    for d in range(1, nh):
        begin(None, remote(sbuf.at[mh], sbuf.at[mh], ss.at[d - 1], sr.at[d - 1], at_h(lax.rem(mh + d, nh))))

    for c in small[2:]:
        c.wait()
    token = lax.broadcasted_iota(jnp.int32, (1, tokens), 1)

    def name_block(b, code):
        named = jnp.where(token % BLK < len_ref[b], owner_ref[b] * reqs + slot_ref[b], -1)
        return jnp.where(token // BLK == b, named, code)

    code = lax.fori_loop(0, tokens // BLK, name_block, jnp.full((1, tokens), -1, jnp.int32))
    cck.wait()
    ccv.wait()
    lane = lax.broadcasted_iota(jnp.int32, (1, 128), 1)
    slots = ckv.shape[2]
    for n in range(reqs):
        skf = sk_ref[n].astype(F32)
        svf = sv_ref[n].astype(F32)
        for g in range(heads):
            cols = slice(g * HD, (g + 1) * HD)
            q = q_ref[g, n * rq : (n + 1) * rq, :]
            s = dot_t(q, ckv[0, n, :, cols]) * scale
            ok = lax.broadcasted_iota(jnp.int32, (1, slots), 1) < clen_ref[n]
            s = jnp.where(ok, s, NEGATIVE)
            m = jnp.max(s, axis=-1, keepdims=True)
            qf = q.astype(F32)
            step = lax.broadcasted_iota(jnp.int32, (rq, 1), 0) // QPK
            own_s = []
            for p in range(steps):
                t = jnp.sum(qf * skf[p : p + 1, cols], axis=-1, keepdims=True) * scale
                t = jnp.where(step >= p, t, NEGATIVE)
                own_s.append(t)
                m = jnp.maximum(m, t)
            w = jnp.where(ok, jnp.exp(s - m), 0.0)
            total = jnp.sum(w, axis=-1, keepdims=True)
            a = jnp.dot(w.astype(BF16), ckv[1, n, :, cols], preferred_element_type=F32)
            for p in range(steps):
                u = jnp.where(step >= p, jnp.exp(own_s[p] - m), 0.0)
                total = total + u
                a = a + u * svf[p : p + 1, cols]
            cst[g, n * rq : (n + 1) * rq, 0:128] = a
            cst[g, n * rq : (n + 1) * rq, 128:256] = jnp.where(lane < 64, m, total)

    count = (nz - 1) * pieces
    xcount = (nx - 1) * xpieces

    def zrelay(i):
        for d in range(2):
            dr = 1 - 2 * d
            chunk = me - dr * (1 + i // pieces)
            good = inside(chunk, nz)
            pl.when(good)(zcopy(d, i, chunk).wait_recv)
            if i + pieces < count:
                begin(jnp.logical_and(good, inside(me + dr, nz)), zcopy(d, i + pieces, chunk))
            part = wbuf.at[chunk, me_g, pl.ds((i % pieces) * wp, wp)]
            begin(good, remote(part, part, ys.at[d, i], yr.at[d, i], peer_g))

    def xrelay(e):
        for d in range(2):
            dr = 1 - 2 * d
            c = chip - dr * (1 + e // xpieces)
            good = inside(c, nx)
            h = c * 2 + core
            pl.when(good)(xcopy(d, e, h).wait_recv)
            if e + xpieces < xcount:
                begin(jnp.logical_and(good, inside(chip + dr, nx)), xcopy(d, e + xpieces, h))
            part = xbuf.at[h, pl.ds((e % xpieces) * tp, tp)]
            begin(good, remote(part, part, cs.at[d, e], cr.at[d, e], at_h(sib)))

    def states_ready():
        remote(xbuf.at[sib], xbuf.at[sib], os_.at[0], or_.at[0], at_h(sib)).wait_recv()
        for e in range(xcount):
            for d in range(2):
                c = chip - (1 - 2 * d) * (1 + e // xpieces)
                part = xbuf.at[c * 2 + 1 - core, pl.ds((e % xpieces) * tp, tp)]
                pl.when(inside(c, nx))(remote(part, part, cs.at[d, e], cr.at[d, e], at_h(sib)).wait_recv)

    def multiply(chunk, k, fresh):
        at = chunk * wr + k * wp
        if wr == xc:
            lhs = xbuf[chunk, :, k * wp : (k + 1) * wp]
        else:
            lhs = xbuf[at // xc, :, pl.ds(pl.multiple_of(at % xc, 128), wp)]
        for j in range(2):
            prod = jnp.dot(lhs, wbuf[chunk, j, pl.ds(k * wp, wp), :], preferred_element_type=F32)
            acc[j] = prod if fresh else acc[j] + prod

    def consume(u):
        if u < pieces:
            multiply(me, u, u == 0)
            return
        i = u - pieces
        for d in range(2):
            chunk = me - (1 - 2 * d) * (1 + i // pieces)

            @pl.when(inside(chunk, nz))
            def _():
                part = wbuf.at[chunk, 1 - me_g, pl.ds((i % pieces) * wp, wp)]
                remote(part, part, ys.at[d, i], yr.at[d, i], peer_g).wait_recv()
                multiply(chunk, i % pieces, False)

    xdue = [max(0, (e + 1) * 2 * count // (3 * xcount) - 1) for e in range(xcount)]
    first = min(max(xdue) + 1, count - 1)
    done = 0
    for i in range(count):
        zrelay(i)
        for e in range(xcount):
            if xdue[e] == i:
                xrelay(e)
        if i == first:
            states_ready()
        if i >= first:
            goal = (pieces + i) * (i - first + 1) // (count - first)
            while done < goal:
                consume(done)
                done += 1
    while done < pieces + count:
        consume(done)
        done += 1

    for d in range(1, nz):
        src = qbuf.at[lax.rem(me - d + nz, nz)]
        remote(src, src, qs.at[d - 1], qr.at[d - 1], at_z(lax.rem(me + d, nz))).wait_recv()
    for d in range(1, nh):
        src = sbuf.at[lax.rem(mh - d + nh, nh)]
        remote(src, src, ss.at[d - 1], sr.at[d - 1], at_h(lax.rem(mh + d, nh))).wait_recv()
    stat = sbuf[0]
    for h in range(1, nh):
        stat = stat + sbuf[h]
    factor = lax.rsqrt(stat[0:1, :] * (1.0 / (nh * xc)) + 1e-05)
    rows = nz * own
    valid = code == lax.broadcasted_iota(jnp.int32, (rows, 1), 0) // rq
    for g in range(heads):
        cols = slice(g * HD, (g + 1) * HD)
        q = qbuf[:, g].reshape(rows, HD)
        s = dot_t(q, acc[0, :, cols].astype(BF16)) * (factor * scale)
        s = jnp.where(valid, s, NEGATIVE)
        m = jnp.max(s, axis=-1, keepdims=True)
        w = jnp.where(valid, jnp.exp(s - m), 0.0)
        total = jnp.sum(w, axis=-1, keepdims=True)
        a = jnp.dot((w * factor).astype(BF16), acc[1, :, cols].astype(BF16), preferred_element_type=F32)
        some = total > 0
        a = a / jnp.where(some, total, 1.0)
        psend[:, g, :, 0:128] = a.astype(BF16).reshape(nz, own, HD)
        both = jnp.where(lane % 2 == 0, m, total)
        big = both.astype(BF16)
        rest = both - big.astype(F32)
        mid = rest.astype(BF16)
        low = (rest - mid.astype(F32)).astype(BF16)
        triple = jnp.where(lane < 32, big.astype(F32), jnp.where(lane < 64, mid.astype(F32), low.astype(F32)))
        psend[:, g, :, 128:256] = triple.astype(BF16).reshape(nz, own, 128)
    for d in range(1, nz):
        to = lax.rem(me + d, nz)
        begin(None, remote(psend.at[to], precv.at[me], ps.at[d - 1], pr.at[d - 1], at_z(to)))
    precv[me] = psend[me]
    for d in range(1, nz):
        src = precv.at[lax.rem(me - d + nz, nz)]
        remote(src, src, ps.at[d - 1], pr.at[d - 1], at_z(lax.rem(me + d, nz))).wait_recv()

    for g in range(heads):
        parts = [(cst[g, :, 0:128], cst[g, :, 128:129], cst[g, :, 192:193], None)]
        for p in range(nz):
            t = precv[p, g].astype(F32)
            m = (t[:, 128:129] + t[:, 160:161]) + t[:, 192:193]
            l = (t[:, 129:130] + t[:, 161:162]) + t[:, 193:194]
            parts.append((t[:, 0:128], m, l, l))
        top = parts[0][1]
        for t in parts[1:]:
            top = jnp.maximum(top, t[1])
        total = jnp.zeros((own, 1), F32)
        a = jnp.zeros((own, HD), F32)
        for t in parts:
            e = jnp.exp(t[1] - top)
            total = total + e * t[2]
            a = a + (e if t[3] is None else e * t[3]) * t[0]
        asend[g] = (a / total).astype(BF16)
    for d in range(1, nz):
        begin(None, remote(asend, arecv.at[me], as_.at[d - 1], ar.at[d - 1], at_z(lax.rem(me + d, nz))))
    arecv[me] = asend[...]
    for d in range(1, nz):
        src = arecv.at[lax.rem(me - d + nz, nz)]
        remote(src, src, as_.at[d - 1], ar.at[d - 1], at_z(lax.rem(me + d, nz))).wait_recv()

    cow.wait()
    for g in range(heads):
        af[g * nz * own : (g + 1) * nz * own, :] = arecv[:, g].reshape(nz * own, HD).astype(F32)
    every = nz * reqs * steps
    pieces_in = [
        af[pl.ds(g * nz * own + j, every, stride=QPK), :] for g in range(heads) for j in range(QPK)
    ]
    lhs = jnp.concatenate(pieces_in, axis=1).astype(BF16)
    prod = jnp.dot(lhs, owbuf[...], preferred_element_type=F32)
    ro = every // nh
    for h in range(nh):
        osend[h] = prod[h * ro : (h + 1) * ro, :]
    for d in range(1, nh):
        to = lax.rem(mh + d, nh)
        begin(None, remote(osend.at[to], orecv.at[mh], fs.at[d - 1], fr.at[d - 1], at_h(to)))
    orecv[mh] = osend[mh]
    for d in range(1, nh):
        src = orecv.at[lax.rem(mh - d + nh, nh)]
        remote(src, src, fs.at[d - 1], fr.at[d - 1], at_h(lax.rem(mh + d, nh))).wait_recv()
    final = orecv[0]
    for h in range(1, nh):
        final = final + orecv[h]
    final = final.astype(BF16)
    for n in range(ro // steps):
        out_ref[n] = final[n * steps : (n + 1) * steps, :]

    for cond, copy in pending:
        if cond is None:
            copy.wait_send()
        else:
            pl.when(cond)(copy.wait_send)


def body(
    prompt_states, norm_gain, key_weight, value_weight, block_owner, block_slot, block_len,
    cache_key, cache_value, cache_len, query, step_key, step_value, out_weight,
):
    nz, nh = lax.axis_size("req"), lax.axis_size("head")
    tokens, xc = prompt_states.shape
    wr, width = key_weight.shape
    heads = width // HD
    reqs, steps = query.shape[0], query.shape[1]
    own = reqs * steps * QPK
    oc = out_weight.shape[1]
    slots = cache_key.shape[1]
    pieces = max(1, wr // 256)
    xpieces = 4
    ro = nz * reqs // nh
    zc = (nz - 1) * pieces
    xcnt = (nh // 2 - 1) * xpieces
    dma = pltpu.SemaphoreType.DMA
    vm = pl.BlockSpec(memory_space=pltpu.VMEM)
    hb = pl.BlockSpec(memory_space=pl.ANY)
    return pl.pallas_call(
        functools.partial(kernel, nz, nh, pieces, xpieces),
        out_shape=jax.ShapeDtypeStruct((ro, steps, oc), BF16),
        in_specs=[hb] * 14,
        out_specs=vm,
        scratch_shapes=[
            pltpu.VMEM(norm_gain.shape, BF16),
            pltpu.SMEM(block_slot.shape, jnp.int32),
            pltpu.SMEM(block_slot.shape, jnp.int32),
            pltpu.SMEM(block_slot.shape, jnp.int32),
            pltpu.SMEM(cache_len.shape, jnp.int32),
            pltpu.VMEM(query.shape, BF16),
            pltpu.VMEM(step_key.shape, BF16),
            pltpu.VMEM(step_value.shape, BF16),
            pltpu.VMEM((heads * own, HD), F32),
            pltpu.VMEM((heads, own, HD), BF16),
            pltpu.VMEM((tokens, xc), BF16),
            pltpu.VMEM((nh, tokens, xc), BF16),
            pltpu.VMEM((nz, 2, wr, width), BF16),
            pltpu.VMEM((2, tokens, width), F32),
            pltpu.VMEM((2, reqs, slots, width), BF16),
            pltpu.VMEM(out_weight.shape, BF16),
            pltpu.VMEM((nz, heads, own, HD), BF16),
            pltpu.VMEM((nz, heads, own, 256), BF16),
            pltpu.VMEM((nz, heads, own, 256), BF16),
            pltpu.VMEM((heads, own, 256), F32),
            pltpu.VMEM((heads, own, HD), BF16),
            pltpu.VMEM((nz, heads, own, HD), BF16),
            pltpu.VMEM((heads * nz * own, HD), F32),
            pltpu.VMEM((nh, ro * steps, oc), F32),
            pltpu.VMEM((nh, ro * steps, oc), F32),
            pltpu.VMEM((nh, 8, tokens), F32),
            dma((14,)),
            dma((2, zc)), dma((2, zc)), dma((2, zc)), dma((2, zc)),
            dma((2, xcnt)), dma((2, xcnt)), dma((2, xcnt)), dma((2, xcnt)),
            dma((1,)), dma((1,)),
            dma((nz - 1,)), dma((nz - 1,)), dma((nz - 1,)), dma((nz - 1,)), dma((nz - 1,)), dma((nz - 1,)),
            dma((nh - 1,)), dma((nh - 1,)), dma((nh - 1,)), dma((nh - 1,)),
        ],
        compiler_params=pltpu.CompilerParams(
            collective_id=0, has_side_effects=True, vmem_limit_bytes=52 * 1024 * 1024
        ),
    )(
        norm_gain, block_owner[:, 0], block_slot, block_len, cache_len, query, step_key, step_value,
        prompt_states, key_weight, value_weight, cache_key, cache_value, out_weight,
    )


def solution(mesh):
    placed = (
        P(("groups", "req"), "head"),
        P(),
        P("req", "head"),
        P("req", "head"),
        P(("groups", "req"), None),
        P(("groups", "req")),
        P(("groups", "req")),
        P(("groups", "req"), None, "head"),
        P(("groups", "req"), None, "head"),
        P(("groups", "req")),
        P(("groups", "req"), None, "head"),
        P(("groups", "req"), None, "head"),
        P(("groups", "req"), None, "head"),
        P("head", "req"),
    )
    return jax.shard_map(
        body,
        mesh=mesh,
        in_specs=placed,
        out_specs=P(("groups", "head"), None, "req"),
        check_vma=False,
    )
```

```python
import functools

import jax
import jax.numpy as jnp
from jax import lax
from jax.experimental import pallas as pl
from jax.experimental.pallas import tpu as pltpu
from jax.sharding import PartitionSpec as P

QPK = 8
HD = 128
BLK = 8
NEGATIVE = -1e30
MESH = pl.DeviceIdType.MESH
F32 = jnp.float32
BF16 = jnp.bfloat16


def dot_t(a, b):
    return lax.dot_general(a, b, (((1,), (1,)), ((), ())), preferred_element_type=F32)


def kernel(
    nz, nh, pieces, xpieces,
    gain_hbm, owner_hbm, slot_hbm, len_hbm, clen_hbm, query_hbm, sk_hbm, sv_hbm,
    x_hbm, wk_hbm, wv_hbm, ck_hbm, cv_hbm, ow_hbm,
    out_ref,
    gain_ref, owner_ref, slot_ref, len_ref, clen_ref, query_ref, sk_ref, sv_ref, qf_ref, q_ref,
    xraw, xbuf, wbuf, acc, ckv, owbuf, qbuf, psend, precv, cst, asend, arecv, af, osend, orecv, sbuf,
    loc, zs, zr, ys, yr, xs, xr, cs, cr, os_, or_, qs, qr, ps, pr, as_, ar, fs, fr, ss, sr,
):
    me_g = lax.axis_index("groups")
    me = lax.axis_index("req")
    mh = lax.axis_index("head")
    chip = mh // 2
    core = mh % 2
    nx = nh // 2
    sib = chip * 2 + (1 - core)
    tokens, xc = xraw.shape
    wr, width = wk_hbm.shape
    heads = width // HD
    wp = wr // pieces
    tp = tokens // xpieces
    reqs, steps = sk_ref.shape[0], sk_ref.shape[1]
    rq = steps * QPK
    own = reqs * rq
    scale = 1.0 / HD**0.5

    def at_z(p):
        return (me_g, p, mh)

    def at_h(h):
        return (me_g, me, h)

    peer_g = (1 - me_g, me, mh)

    def remote(src, dst, ssem, rsem, dev):
        return pltpu.make_async_remote_copy(
            src_ref=src, dst_ref=dst, send_sem=ssem, recv_sem=rsem, device_id=dev, device_id_type=MESH
        )

    cpx = pltpu.make_async_copy(x_hbm, xraw, loc.at[0])
    cpk = pltpu.make_async_copy(wk_hbm, wbuf.at[me, 0], loc.at[1])
    cpv = pltpu.make_async_copy(wv_hbm, wbuf.at[me, 1], loc.at[2])
    cck = pltpu.make_async_copy(ck_hbm, ckv.at[0], loc.at[3])
    ccv = pltpu.make_async_copy(cv_hbm, ckv.at[1], loc.at[4])
    cow = pltpu.make_async_copy(ow_hbm, owbuf, loc.at[5])
    small = [
        pltpu.make_async_copy(src, dst, loc.at[6 + i])
        for i, (src, dst) in enumerate(
            [
                (query_hbm, query_ref), (gain_hbm, gain_ref), (owner_hbm, owner_ref), (slot_hbm, slot_ref),
                (len_hbm, len_ref), (clen_hbm, clen_ref), (sk_hbm, sk_ref), (sv_hbm, sv_ref),
            ]
        )
    ]
    for c in (cpk, cpv, cpx, *small, cck, ccv, cow):
        c.start()

    barrier = pltpu.get_barrier_semaphore()
    for d in range(1, nz):
        pl.semaphore_signal(barrier, inc=1, device_id=at_z(lax.rem(me + d, nz)), device_id_type=MESH)
    for d in range(1, nh):
        pl.semaphore_signal(barrier, inc=1, device_id=at_h(lax.rem(mh + d, nh)), device_id_type=MESH)
    pl.semaphore_signal(barrier, inc=1, device_id=peer_g, device_id_type=MESH)
    pl.semaphore_wait(barrier, nz + nh - 1)

    pending = []

    def begin(cond, copy):
        pending.append((cond, copy))
        if cond is None:
            copy.start()
        else:
            pl.when(cond)(copy.start)

    def zcopy(d, i, chunk):
        dr = 1 - 2 * d
        k = i % pieces
        part = wbuf.at[chunk, me_g, pl.ds(k * wp, wp)]
        return remote(part, part, zs.at[d, i], zr.at[d, i], at_z(me + dr))

    def inside(v, n):
        return jnp.logical_and(v >= 0, v < n)

    cpk.wait()
    cpv.wait()
    for k in range(pieces):
        for d in range(2):
            begin(inside(me + 1 - 2 * d, nz), zcopy(d, k, me))

    small[0].wait()
    for n in range(reqs):
        both = query_ref[n].astype(F32)
        for g in range(heads):
            for j in range(QPK):
                lanes = (g * QPK + j) * HD
                qf_ref[pl.ds(g * own + n * rq + j, steps, stride=QPK), :] = both[:, lanes : lanes + HD]
    q_ref[...] = qf_ref[...].astype(BF16).reshape(heads, own, HD)
    for d in range(1, nz):
        begin(None, remote(q_ref, qbuf.at[me], qs.at[d - 1], qr.at[d - 1], at_z(lax.rem(me + d, nz))))
    qbuf[me] = q_ref[...]

    cpx.wait()
    small[1].wait()
    gain = gain_ref[pl.ds(pl.multiple_of(mh * xc, 128), xc)].astype(F32).reshape(1, xc)

    def xcopy(d, e, c):
        dr = 1 - 2 * d
        k = e % xpieces
        part = xbuf.at[c, pl.ds(k * tp, tp)]
        return remote(part, part, xs.at[d, e], xr.at[d, e], at_h(mh + 2 * dr))

    ones = jnp.ones((8, xc), BF16)
    for k in range(xpieces):
        rows = pl.ds(k * tp, tp)
        xf = xraw[rows, :].astype(F32)
        xbuf[mh, rows, :] = (xf * gain).astype(BF16)
        for d in range(2):
            begin(inside(chip + 1 - 2 * d, nx), xcopy(d, k, mh))
        sq = xf * xf
        hi = sq.astype(BF16)
        lo = (sq - hi.astype(F32)).astype(BF16)
        sbuf[mh, :, k * tp : (k + 1) * tp] = dot_t(ones, hi) + dot_t(ones, lo)
    begin(None, remote(xbuf.at[mh], xbuf.at[mh], os_.at[0], or_.at[0], at_h(sib)))
    for d in range(1, nh):
        begin(None, remote(sbuf.at[mh], sbuf.at[mh], ss.at[d - 1], sr.at[d - 1], at_h(lax.rem(mh + d, nh))))

    for c in small[2:]:
        c.wait()
    token = lax.broadcasted_iota(jnp.int32, (1, tokens), 1)

    def name_block(b, code):
        named = jnp.where(token % BLK < len_ref[b], owner_ref[b] * reqs + slot_ref[b], -1)
        return jnp.where(token // BLK == b, named, code)

    code = lax.fori_loop(0, tokens // BLK, name_block, jnp.full((1, tokens), -1, jnp.int32))
    cck.wait()
    ccv.wait()
    lane = lax.broadcasted_iota(jnp.int32, (1, 128), 1)
    slots = ckv.shape[2]
    for n in range(reqs):
        skf = sk_ref[n].astype(F32)
        svf = sv_ref[n].astype(F32)
        for g in range(heads):
            cols = slice(g * HD, (g + 1) * HD)
            q = q_ref[g, n * rq : (n + 1) * rq, :]
            s = dot_t(q, ckv[0, n, :, cols]) * scale
            ok = lax.broadcasted_iota(jnp.int32, (1, slots), 1) < clen_ref[n]
            s = jnp.where(ok, s, NEGATIVE)
            m = jnp.max(s, axis=-1, keepdims=True)
            qf = q.astype(F32)
            step = lax.broadcasted_iota(jnp.int32, (rq, 1), 0) // QPK
            own_s = []
            for p in range(steps):
                t = jnp.sum(qf * skf[p : p + 1, cols], axis=-1, keepdims=True) * scale
                t = jnp.where(step >= p, t, NEGATIVE)
                own_s.append(t)
                m = jnp.maximum(m, t)
            w = jnp.where(ok, jnp.exp(s - m), 0.0)
            total = jnp.sum(w, axis=-1, keepdims=True)
            a = jnp.dot(w.astype(BF16), ckv[1, n, :, cols], preferred_element_type=F32)
            for p in range(steps):
                u = jnp.where(step >= p, jnp.exp(own_s[p] - m), 0.0)
                total = total + u
                a = a + u * svf[p : p + 1, cols]
            cst[g, n * rq : (n + 1) * rq, 0:128] = a
            cst[g, n * rq : (n + 1) * rq, 128:256] = jnp.where(lane < 64, m, total)

    count = (nz - 1) * pieces
    xcount = (nx - 1) * xpieces

    def zrelay(i):
        for d in range(2):
            dr = 1 - 2 * d
            chunk = me - dr * (1 + i // pieces)
            good = inside(chunk, nz)
            pl.when(good)(zcopy(d, i, chunk).wait_recv)
            if i + pieces < count:
                begin(jnp.logical_and(good, inside(me + dr, nz)), zcopy(d, i + pieces, chunk))
            part = wbuf.at[chunk, me_g, pl.ds((i % pieces) * wp, wp)]
            begin(good, remote(part, part, ys.at[d, i], yr.at[d, i], peer_g))

    def xrelay(e):
        for d in range(2):
            dr = 1 - 2 * d
            c = chip - dr * (1 + e // xpieces)
            good = inside(c, nx)
            h = c * 2 + core
            pl.when(good)(xcopy(d, e, h).wait_recv)
            if e + xpieces < xcount:
                begin(jnp.logical_and(good, inside(chip + dr, nx)), xcopy(d, e + xpieces, h))
            part = xbuf.at[h, pl.ds((e % xpieces) * tp, tp)]
            begin(good, remote(part, part, cs.at[d, e], cr.at[d, e], at_h(sib)))

    def states_ready():
        remote(xbuf.at[sib], xbuf.at[sib], os_.at[0], or_.at[0], at_h(sib)).wait_recv()
        for e in range(xcount):
            for d in range(2):
                c = chip - (1 - 2 * d) * (1 + e // xpieces)
                part = xbuf.at[c * 2 + 1 - core, pl.ds((e % xpieces) * tp, tp)]
                pl.when(inside(c, nx))(remote(part, part, cs.at[d, e], cr.at[d, e], at_h(sib)).wait_recv)

    def multiply(chunk, k, fresh):
        at = chunk * wr + k * wp
        if wr == xc:
            lhs = xbuf[chunk, :, k * wp : (k + 1) * wp]
        else:
            lhs = xbuf[at // xc, :, pl.ds(pl.multiple_of(at % xc, 128), wp)]
        for j in range(2):
            prod = jnp.dot(lhs, wbuf[chunk, j, pl.ds(k * wp, wp), :], preferred_element_type=F32)
            acc[j] = prod if fresh else acc[j] + prod

    def consume(u):
        if u < pieces:
            multiply(me, u, u == 0)
            return
        i = u - pieces
        for d in range(2):
            chunk = me - (1 - 2 * d) * (1 + i // pieces)

            @pl.when(inside(chunk, nz))
            def _():
                part = wbuf.at[chunk, 1 - me_g, pl.ds((i % pieces) * wp, wp)]
                remote(part, part, ys.at[d, i], yr.at[d, i], peer_g).wait_recv()
                multiply(chunk, i % pieces, False)

    xdue = [max(0, (e + 1) * 2 * count // (3 * xcount) - 1) for e in range(xcount)]
    first = min(max(xdue) + 1, count - 1)
    done = 0
    for i in range(count):
        zrelay(i)
        for e in range(xcount):
            if xdue[e] == i:
                xrelay(e)
        if i == first:
            states_ready()
        if i >= first:
            goal = (pieces + i) * (i - first + 1) // (count - first)
            while done < goal:
                consume(done)
                done += 1
    while done < pieces + count:
        consume(done)
        done += 1

    for d in range(1, nz):
        src = qbuf.at[lax.rem(me - d + nz, nz)]
        remote(src, src, qs.at[d - 1], qr.at[d - 1], at_z(lax.rem(me + d, nz))).wait_recv()
    for d in range(1, nh):
        src = sbuf.at[lax.rem(mh - d + nh, nh)]
        remote(src, src, ss.at[d - 1], sr.at[d - 1], at_h(lax.rem(mh + d, nh))).wait_recv()
    stat = sbuf[0]
    for h in range(1, nh):
        stat = stat + sbuf[h]
    factor = lax.rsqrt(stat[0:1, :] * (1.0 / (nh * xc)) + 1e-05)
    rows = nz * own
    valid = code == lax.broadcasted_iota(jnp.int32, (rows, 1), 0) // rq
    for g in range(heads):
        cols = slice(g * HD, (g + 1) * HD)
        q = qbuf[:, g].reshape(rows, HD)
        s = dot_t(q, acc[0, :, cols].astype(BF16)) * (factor * scale)
        s = jnp.where(valid, s, NEGATIVE)
        m = jnp.max(s, axis=-1, keepdims=True)
        w = jnp.where(valid, jnp.exp(s - m), 0.0)
        total = jnp.sum(w, axis=-1, keepdims=True)
        a = jnp.dot((w * factor).astype(BF16), acc[1, :, cols].astype(BF16), preferred_element_type=F32)
        some = total > 0
        a = a / jnp.where(some, total, 1.0)
        psend[:, g, :, 0:128] = a.astype(BF16).reshape(nz, own, HD)
        both = jnp.where(lane % 2 == 0, m, total)
        big = both.astype(BF16)
        rest = both - big.astype(F32)
        mid = rest.astype(BF16)
        low = (rest - mid.astype(F32)).astype(BF16)
        triple = jnp.where(lane < 32, big.astype(F32), jnp.where(lane < 64, mid.astype(F32), low.astype(F32)))
        psend[:, g, :, 128:256] = triple.astype(BF16).reshape(nz, own, 128)
        for d in range(1, nz):
            to = lax.rem(me + d, nz)
            begin(None, remote(psend.at[to, g], precv.at[me, g], ps.at[d - 1, g], pr.at[d - 1, g], at_z(to)))
        precv[me, g] = psend[me, g]

    for g in range(heads):
        for d in range(1, nz):
            src = precv.at[lax.rem(me - d + nz, nz), g]
            remote(src, src, ps.at[d - 1, g], pr.at[d - 1, g], at_z(lax.rem(me + d, nz))).wait_recv()
        parts = [(cst[g, :, 0:128], cst[g, :, 128:129], cst[g, :, 192:193], None)]
        for p in range(nz):
            t = precv[p, g].astype(F32)
            m = (t[:, 128:129] + t[:, 160:161]) + t[:, 192:193]
            l = (t[:, 129:130] + t[:, 161:162]) + t[:, 193:194]
            parts.append((t[:, 0:128], m, l, l))
        top = parts[0][1]
        for t in parts[1:]:
            top = jnp.maximum(top, t[1])
        total = jnp.zeros((own, 1), F32)
        a = jnp.zeros((own, HD), F32)
        for t in parts:
            e = jnp.exp(t[1] - top)
            total = total + e * t[2]
            a = a + (e if t[3] is None else e * t[3]) * t[0]
        asend[g] = (a / total).astype(BF16)
        for d in range(1, nz):
            to = at_z(lax.rem(me + d, nz))
            begin(None, remote(asend.at[g], arecv.at[me, g], as_.at[d - 1, g], ar.at[d - 1, g], to))
        arecv[me, g] = asend[g]

    cow.wait()
    for g in range(heads):
        for d in range(1, nz):
            src = arecv.at[lax.rem(me - d + nz, nz), g]
            remote(src, src, as_.at[d - 1, g], ar.at[d - 1, g], at_z(lax.rem(me + d, nz))).wait_recv()
        af[g * nz * own : (g + 1) * nz * own, :] = arecv[:, g].reshape(nz * own, HD).astype(F32)
    every = nz * reqs * steps
    pieces_in = [
        af[pl.ds(g * nz * own + j, every, stride=QPK), :] for g in range(heads) for j in range(QPK)
    ]
    lhs = jnp.concatenate(pieces_in, axis=1).astype(BF16)
    prod = jnp.dot(lhs, owbuf[...], preferred_element_type=F32)
    ro = every // nh
    for h in range(nh):
        osend[h] = prod[h * ro : (h + 1) * ro, :]
    for d in range(1, nh):
        to = lax.rem(mh + d, nh)
        begin(None, remote(osend.at[to], orecv.at[mh], fs.at[d - 1], fr.at[d - 1], at_h(to)))
    orecv[mh] = osend[mh]
    for d in range(1, nh):
        src = orecv.at[lax.rem(mh - d + nh, nh)]
        remote(src, src, fs.at[d - 1], fr.at[d - 1], at_h(lax.rem(mh + d, nh))).wait_recv()
    final = orecv[0]
    for h in range(1, nh):
        final = final + orecv[h]
    final = final.astype(BF16)
    for n in range(ro // steps):
        out_ref[n] = final[n * steps : (n + 1) * steps, :]

    for cond, copy in pending:
        if cond is None:
            copy.wait_send()
        else:
            pl.when(cond)(copy.wait_send)


def body(
    prompt_states, norm_gain, key_weight, value_weight, block_owner, block_slot, block_len,
    cache_key, cache_value, cache_len, query, step_key, step_value, out_weight,
):
    nz, nh = lax.axis_size("req"), lax.axis_size("head")
    tokens, xc = prompt_states.shape
    wr, width = key_weight.shape
    heads = width // HD
    reqs, steps = query.shape[0], query.shape[1]
    own = reqs * steps * QPK
    oc = out_weight.shape[1]
    slots = cache_key.shape[1]
    pieces = max(1, wr // 256)
    xpieces = 4
    ro = nz * reqs // nh
    zc = (nz - 1) * pieces
    xcnt = (nh // 2 - 1) * xpieces
    dma = pltpu.SemaphoreType.DMA
    vm = pl.BlockSpec(memory_space=pltpu.VMEM)
    hb = pl.BlockSpec(memory_space=pltpu.HBM)
    return pl.pallas_call(
        functools.partial(kernel, nz, nh, pieces, xpieces),
        out_shape=jax.ShapeDtypeStruct((ro, steps, oc), BF16),
        in_specs=[hb] * 14,
        out_specs=vm,
        scratch_shapes=[
            pltpu.VMEM(norm_gain.shape, BF16),
            pltpu.SMEM(block_slot.shape, jnp.int32),
            pltpu.SMEM(block_slot.shape, jnp.int32),
            pltpu.SMEM(block_slot.shape, jnp.int32),
            pltpu.SMEM(cache_len.shape, jnp.int32),
            pltpu.VMEM(query.shape, BF16),
            pltpu.VMEM(step_key.shape, BF16),
            pltpu.VMEM(step_value.shape, BF16),
            pltpu.VMEM((heads * own, HD), F32),
            pltpu.VMEM((heads, own, HD), BF16),
            pltpu.VMEM((tokens, xc), BF16),
            pltpu.VMEM((nh, tokens, xc), BF16),
            pltpu.VMEM((nz, 2, wr, width), BF16),
            pltpu.VMEM((2, tokens, width), F32),
            pltpu.VMEM((2, reqs, slots, width), BF16),
            pltpu.VMEM(out_weight.shape, BF16),
            pltpu.VMEM((nz, heads, own, HD), BF16),
            pltpu.VMEM((nz, heads, own, 256), BF16),
            pltpu.VMEM((nz, heads, own, 256), BF16),
            pltpu.VMEM((heads, own, 256), F32),
            pltpu.VMEM((heads, own, HD), BF16),
            pltpu.VMEM((nz, heads, own, HD), BF16),
            pltpu.VMEM((heads * nz * own, HD), F32),
            pltpu.VMEM((nh, ro * steps, oc), F32),
            pltpu.VMEM((nh, ro * steps, oc), F32),
            pltpu.VMEM((nh, 8, tokens), F32),
            dma((14,)),
            dma((2, zc)), dma((2, zc)), dma((2, zc)), dma((2, zc)),
            dma((2, xcnt)), dma((2, xcnt)), dma((2, xcnt)), dma((2, xcnt)),
            dma((1,)), dma((1,)),
            dma((nz - 1,)), dma((nz - 1,)), dma((nz - 1, heads)), dma((nz - 1, heads)), dma((nz - 1, heads)), dma((nz - 1, heads)),
            dma((nh - 1,)), dma((nh - 1,)), dma((nh - 1,)), dma((nh - 1,)),
        ],
        compiler_params=pltpu.CompilerParams(
            collective_id=0, has_side_effects=True, vmem_limit_bytes=52 * 1024 * 1024
        ),
    )(
        norm_gain, block_owner[:, 0], block_slot, block_len, cache_len, query, step_key, step_value,
        prompt_states, key_weight, value_weight, cache_key, cache_value, out_weight,
    )


def solution(mesh):
    placed = (
        P(("groups", "req"), "head"),
        P(),
        P("req", "head"),
        P("req", "head"),
        P(("groups", "req"), None),
        P(("groups", "req")),
        P(("groups", "req")),
        P(("groups", "req"), None, "head"),
        P(("groups", "req"), None, "head"),
        P(("groups", "req")),
        P(("groups", "req"), None, "head"),
        P(("groups", "req"), None, "head"),
        P(("groups", "req"), None, "head"),
        P("head", "req"),
    )
    return jax.shard_map(
        body,
        mesh=mesh,
        in_specs=placed,
        out_specs=P(("groups", "head"), None, "req"),
        check_vma=False,
    )
```
